32 devices in a mesh: tm: 4 (over z), strip: 8 (over y, x, core).
Axes of the slice: x: 2, y: 2, z: 4, core: 2. Of those that a mesh axis runs over, the one named last changes fastest.
Arguments:
- prev_states: float32 [4, 4, 64, 384], P('tm', None, 'strip'), may hold values from -6 to 6
- observation: bfloat16 [4, 64, 384], P(None, 'strip'), may hold values from -6 to 6
- bounds: int32 [5], replicated, may hold values from 0 to 1000, as said below
- coarse_factor: float32 [4, 4], replicated, may hold values from 0 to 1, as said below
- time_weight: float32 [64], replicated, may hold values from -6 to 6
- weight_in: bfloat16 [3, 3, 64, 8], replicated, may hold values from -1 to 1
- weight_mid: bfloat16 [4, 3, 3, 64, 64], replicated, may hold values from -0.375 to 0.375
- weight_out: bfloat16 [3, 3, 4, 64], replicated, may hold values from -0.375 to 0.375
Outputs:
- new_states: float32 [4, 4, 64, 384], P('tm', None, 'strip')
The draws below stay inside these ranges and needn't reach their ends.
Inputs may be any that keep to these rules, and one draw needn't show every extreme that they name: bounds[0] = 0, bounds[4] = 1000, strictly increasing. `coarse_factor`: every factor lies strictly between 0 and 1.
All inputs are finite; a program needn't handle non-finite values.
Results may differ from the reference program's by a relative error of at most 0.002.
Values may be sent and summed in bfloat16 or wider, within the bound.
A program may use at most 64 MiB of HBM per device.

```python
import jax
import jax.numpy as jnp
from jax import lax

HIDDEN_FEATURES = 4
HID = 64
LAYERS = 6
STEPS = 1000
COLS = 384
INTERVAL_COUNT = 4
HEIGHT = 64


def draw_bounds(key, part):
    inner = jax.random.permutation(key, STEPS - 1)[:INTERVAL_COUNT - 1] + 1
    inner = jnp.sort(inner.astype(jnp.int32))
    return jnp.concatenate([jnp.zeros((1,), jnp.int32), inner, jnp.full((1,), STEPS, jnp.int32)])


def draw_coarse_factor(key, part):
    selector_seed, speed_seed, jitter_seed, surge_seed, stack_seed = jax.random.split(key, 5)
    slowly = jax.random.permutation(selector_seed, HIDDEN_FEATURES) < HIDDEN_FEATURES // 2
    slow_rate = 0.6 / INTERVAL_COUNT
    fast_rates = jnp.exp(jax.random.uniform(speed_seed, (HIDDEN_FEATURES,), jnp.float32, jnp.log(0.5), jnp.log(1.5)))
    speed_options = jnp.where(slowly, slow_rate, fast_rates)
    jitter_magnitude = jax.random.uniform(jitter_seed, (INTERVAL_COUNT, HIDDEN_FEATURES), jnp.float32, 0.5, 1.5)
    surge_durations = jax.random.uniform(surge_seed, (INTERVAL_COUNT, HIDDEN_FEATURES), jnp.float32) < 2.0 / INTERVAL_COUNT
    stack_heights = jax.random.uniform(stack_seed, (INTERVAL_COUNT, HIDDEN_FEATURES), jnp.float32, 0.6, 0.8)
    return jnp.exp(-speed_options[None, :] * jitter_magnitude) * jnp.where(surge_durations, stack_heights, 1.0)


def steps_of(key, shape, shards, smallest, largest):
    level = 1.0
    for axis_at, shards_of in shards:
        steps = jax.random.uniform(jax.random.fold_in(jax.random.fold_in(key, 6), axis_at), (shards_of,), jnp.float32, smallest / len(shards), largest / len(shards))
        level = level * jnp.repeat(jnp.exp(steps), shape[axis_at] // shards_of).reshape((-1,) + (1,) * (len(shape) - 1 - axis_at))
    return level


def scatter_about(key, extent, scale, reach, cuts=(), kind=jnp.bfloat16):
    values = scale * jax.random.normal(key, extent, jnp.float32)
    if cuts:
        values = values * steps_of(key, extent, cuts, -0.22, 0.18)
    return jnp.clip(values, -reach, reach).astype(kind)


def setup_inputs(seed: int = 0) -> dict:
    key_list = jax.random.split(jax.random.key(seed), 9)
    prev_states = scatter_about(key_list[0], (INTERVAL_COUNT, HIDDEN_FEATURES, HEIGHT, COLS), 1.0, 6.0, ((0, 4), (2, 8)), jnp.float32)
    observation = scatter_about(key_list[1], (HIDDEN_FEATURES, HEIGHT, COLS), 1.0, 6.0, ((1, 8),))
    bounds = draw_bounds(jax.random.fold_in(key_list[8], 71), 0)
    coarse_factor = draw_coarse_factor(jax.random.fold_in(key_list[8], 71), 0)
    time_weight = scatter_about(key_list[4], (HID,), 1.0, 6.0, (), jnp.float32)
    weight_in = scatter_about(key_list[5], (3, 3, HID, 2 * HIDDEN_FEATURES), (9 * HIDDEN_FEATURES) ** -0.5, 1.0)
    weight_mid = scatter_about(key_list[6], (LAYERS - 2, 3, 3, HID, HID), (9 * HID // 2) ** -0.5, 0.375)
    weight_out = scatter_about(key_list[7], (3, 3, HIDDEN_FEATURES, HID), (9 * HID // 2) ** -0.5, 0.375)
    return dict(prev_states=prev_states, observation=observation, bounds=bounds, coarse_factor=coarse_factor, time_weight=time_weight, weight_in=weight_in, weight_mid=weight_mid, weight_out=weight_out)


def convolve(layer_in, weight):
    kernel = jnp.transpose(weight, (2, 3, 0, 1)).astype(jnp.float32)
    summed = lax.conv_general_dilated(layer_in.astype(jnp.float32)[None], kernel, (1, 1), ((1, 1), (1, 1)), dimension_numbers=("NCHW", "OIHW", "NCHW"), precision=lax.Precision.HIGHEST)
    return summed[0]


def velocity_of(state, observation, time_now, time_weight, weight_in, weight_mid, weight_out):
    features = jnp.concatenate([state.astype(jnp.bfloat16), observation], axis=0)
    hidden = jax.nn.silu(convolve(features, weight_in) + time_now * time_weight[:, None, None]).astype(jnp.bfloat16)
    for level in range(LAYERS - 2):
        hidden = jax.nn.silu(convolve(hidden, weight_mid[level])).astype(jnp.bfloat16)
    return convolve(hidden, weight_out)


def reference(prev_states, observation, bounds, coarse_factor, time_weight, weight_in, weight_mid, weight_out):
    def one_slice(packed):
        state, factor, begin, finish, index = packed
        time_now = begin.astype(jnp.float32) / STEPS
        time_step = (finish - begin).astype(jnp.float32) / STEPS
        velocity = velocity_of(state, observation, time_now, time_weight, weight_in, weight_mid, weight_out)
        fine = state + time_step * velocity
        keeper = (index != 0).astype(jnp.float32)
        return fine - keeper * factor[:, None, None] * state

    indices = jnp.arange(INTERVAL_COUNT).astype(jnp.int32)
    jumps = lax.map(one_slice, (prev_states, coarse_factor, bounds[:-1], bounds[1:], indices))

    def advance(carried, packed):
        factor, jump = packed
        result = factor[:, None, None] * carried + jump
        return result, result

    start = jnp.zeros(prev_states.shape[1:], jnp.float32)
    ignored, new_states = lax.scan(advance, start, (coarse_factor, jumps))
    return new_states
```

```python
import functools

import jax
import jax.numpy as jnp
from jax import lax
from jax.experimental import pallas as pl
from jax.experimental.pallas import tpu as pltpu
from jax.sharding import PartitionSpec as P

STEPS = 1000
MESH = pl.DeviceIdType.MESH
F32 = jnp.float32
BF16 = jnp.bfloat16


def kernel(
    slices,
    strips,
    prev_ref,
    obs_ref,
    bounds_ref,
    factor_ref,
    time_ref,
    win_ref,
    wmid_ref,
    wout_ref,
    out_ref,
    own,
    above,
    below,
    field,
    w_first,
    w_mid,
    w_last,
    hidden_a,
    hidden_b,
    arrived,
    halo_send,
    halo_recv,
    relay_send,
    relay_recv,
):
    t = lax.axis_index("tm")
    s = lax.axis_index("strip")
    channels, rows, cols = prev_ref.shape[1:]
    hid = time_ref.shape[1]
    middle = wmid_ref.shape[0]
    not_top, not_bottom = s > 0, s < strips - 1
    not_first, not_last = t > 0, t < slices - 1

    barrier = pltpu.get_barrier_semaphore()

    def greet(tt, ss):
        pl.semaphore_signal(barrier, inc=1, device_id=(tt, ss), device_id_type=MESH)

    pl.when(not_top)(lambda: greet(t, s - 1))
    pl.when(not_bottom)(lambda: greet(t, s + 1))
    pl.when(not_first)(lambda: greet(t - 1, s))
    pl.when(not_last)(lambda: greet(t + 1, s))

    for c in range(channels):
        field[c, rows : 2 * rows, :] = prev_ref[0, c]
        field[channels + c, rows : 2 * rows, :] = obs_ref[c].astype(F32)
    own[...] = field[:, rows : 2 * rows, :].reshape(2 * channels * rows, cols).astype(BF16)

    greeted = (
        not_top.astype(jnp.int32)
        + not_bottom.astype(jnp.int32)
        + not_first.astype(jnp.int32)
        + not_last.astype(jnp.int32)
    )
    pl.semaphore_wait(barrier, greeted)

    def to_above():
        return pltpu.make_async_remote_copy(
            own, below, halo_send.at[0], halo_recv.at[1], (t, s - 1), MESH
        )

    def to_below():
        return pltpu.make_async_remote_copy(
            own, above, halo_send.at[1], halo_recv.at[0], (t, s + 1), MESH
        )

    pl.when(not_top)(lambda: to_above().start())
    pl.when(not_bottom)(lambda: to_below().start())

    lane = lax.broadcasted_iota(jnp.int32, (2 * channels, 256), 1)
    chan = lax.broadcasted_iota(jnp.int32, (2 * channels, 256), 0)
    base = jnp.zeros((hid, 256), F32)
    for i in range(3):
        for j in range(3):
            pick = (lane == j * 64 + chan * 8 + i).astype(F32).astype(BF16)
            base = base + jnp.dot(win_ref[i, j], pick, preferred_element_type=F32)
    base = base * 0.5
    for b in range(6):
        turned = pltpu.roll(base, b, 1) if b else base
        w_first[b * hid : (b + 1) * hid, :] = turned.astype(BF16)

    half = jnp.asarray(0.5, BF16)
    none = jnp.zeros((hid, hid), BF16)
    for level in range(middle):
        for j in range(3):
            w = [wmid_ref[level, i, j] * half for i in range(3)]
            at = 2 * j * hid
            w_mid[level, at : at + hid, :] = jnp.concatenate(w + [none], axis=1)
            w_mid[level, at + hid : at + 2 * hid, :] = jnp.concatenate([none] + w, axis=1)

    block = lax.broadcasted_iota(jnp.int32, (rows, 128), 1) // hid
    row_at = lax.broadcasted_iota(jnp.int32, (rows, 128), 0)
    for j in range(3):
        taps = []
        for i in range(3):
            tap = wout_ref[i, j].astype(F32)
            taps.append(jnp.concatenate([tap, tap], axis=1))
        for tile in range((rows + 2) * hid // 128):
            diff = block + 2 * tile - row_at
            parts = []
            for o in range(channels):
                part = jnp.zeros((rows, 128), F32)
                for i in range(3):
                    spread = jnp.broadcast_to(taps[i][o : o + 1], (rows, 128))
                    part = jnp.where(diff == i, spread, part)
                parts.append(part)
            w_last[
                j * channels * rows : (j + 1) * channels * rows, tile * 128 : (tile + 1) * 128
            ] = jnp.concatenate(parts, axis=0).astype(BF16)

    begin = bounds_ref[t].astype(F32)
    finish = bounds_ref[t + 1].astype(F32)
    time_now = begin / STEPS
    time_step = (finish - begin) / STEPS
    eye = lax.broadcasted_iota(jnp.int32, (hid, hid), 0) == lax.broadcasted_iota(
        jnp.int32, (hid, hid), 1
    )
    spread = jnp.broadcast_to(time_ref[...], (hid, hid))
    column = jnp.sum(jnp.where(eye, spread, 0.0), axis=1, keepdims=True)
    bias = (0.5 * time_now) * column

    keep_top = not_top.astype(F32)
    keep_bottom = not_bottom.astype(F32)

    def activated(u, row):
        h = u + u * jnp.tanh(u)
        if row < rows:
            h = h * keep_top
        elif row >= 2 * rows:
            h = h * keep_bottom
        return h.astype(BF16)

    def from_left(v):
        at = lax.broadcasted_iota(jnp.int32, v.shape, 1)
        return jnp.where(at == 0, 0.0, pltpu.roll(v, 1, 1))

    def from_right(v):
        at = lax.broadcasted_iota(jnp.int32, v.shape, 1)
        return jnp.where(at == cols - 1, 0.0, pltpu.roll(v, cols - 1, 1))

    def first_layer(group):
        start = 2 + 6 * group
        window = field[:, start : start + 8, :].reshape(16 * channels, cols)
        stacked = jnp.concatenate(
            [from_left(window).astype(BF16), window.astype(BF16), from_right(window).astype(BF16)],
            axis=0,
        )
        got = jnp.dot(w_first[:, : 3 * 64], stacked, preferred_element_type=F32)
        for b in range(6):
            u = got[b * hid : (b + 1) * hid] + bias
            at = (6 * group + b) * hid
            hidden_a[at : at + hid, :] = activated(u, start + 1 + b)

    first_layer(1)

    @pl.when(not_top)
    def _():
        to_above().wait_send()
        to_below_recv = pltpu.make_async_remote_copy(
            own, above, halo_send.at[1], halo_recv.at[0], (t, s - 1), MESH
        )
        to_below_recv.wait_recv()

    @pl.when(not_bottom)
    def _():
        to_below().wait_send()
        to_above_recv = pltpu.make_async_remote_copy(
            own, below, halo_send.at[0], halo_recv.at[1], (t, s + 1), MESH
        )
        to_above_recv.wait_recv()

    @pl.when(s == 0)
    def _():
        above[...] = jnp.zeros_like(above)

    @pl.when(s == strips - 1)
    def _():
        below[...] = jnp.zeros_like(below)

    field[:, :rows, :] = above[...].astype(F32).reshape(2 * channels, rows, cols)
    field[:, 2 * rows : 3 * rows, :] = below[...].astype(F32).reshape(2 * channels, rows, cols)
    first_layer(0)
    first_layer(2)

    source, target = hidden_a, hidden_b
    for level in range(middle):
        pairs = 8 - level
        for p in range(pairs):
            got = jnp.dot(
                w_mid[level],
                source[p * 2 * hid : p * 2 * hid + 4 * hid, :],
                preferred_element_type=F32,
            )
            u = (
                from_left(got[: 2 * hid])
                + got[2 * hid : 4 * hid]
                + from_right(got[4 * hid :])
            )
            for b in range(2):
                at = (2 * p + b) * hid
                target[at : at + hid, :] = activated(
                    u[b * hid : (b + 1) * hid], 4 + level + 2 * p + b
                )
        source, target = target, source

    count = channels * rows
    got = jnp.dot(w_last[...], source[: (rows + 2) * hid, :], preferred_element_type=F32)
    velocity = from_left(got[:count]) + got[count : 2 * count] + from_right(got[2 * count :])

    def onward(c):
        return pltpu.make_async_remote_copy(
            out_ref.at[0, c], arrived.at[c], relay_send.at[c], relay_recv.at[c], (t + 1, s), MESH
        )

    def backward(c):
        return pltpu.make_async_remote_copy(
            out_ref.at[0, c], arrived.at[c], relay_send.at[c], relay_recv.at[c], (t - 1, s), MESH
        )

    for c in range(channels):
        state = prev_ref[0, c]
        out_ref[0, c] = state + time_step * velocity[c * rows : (c + 1) * rows]

    for c in range(channels):

        @pl.when(not_first)
        def _():
            backward(c).wait_recv()
            out_ref[0, c] = out_ref[0, c] + factor_ref[t, c] * (arrived[c] - prev_ref[0, c])

        pl.when(not_last)(lambda: onward(c).start())

    @pl.when(not_last)
    def _():
        for c in range(channels):
            onward(c).wait_send()


def on_device(slices, strips, *args):
    prev, obs, bounds, factor, time_weight, win, wmid, wout = args
    channels, rows, cols = prev.shape[1:]
    hid = time_weight.shape[0]
    vmem = pl.BlockSpec(memory_space=pltpu.VMEM)
    smem = pl.BlockSpec(memory_space=pltpu.SMEM)
    return pl.pallas_call(
        functools.partial(kernel, slices, strips),
        out_shape=jax.ShapeDtypeStruct(prev.shape, F32),
        in_specs=[vmem, vmem, smem, smem, vmem, vmem, vmem, vmem],
        out_specs=vmem,
        scratch_shapes=[
            pltpu.VMEM((2 * channels * rows, cols), BF16),
            pltpu.VMEM((2 * channels * rows, cols), BF16),
            pltpu.VMEM((2 * channels * rows, cols), BF16),
            pltpu.VMEM((2 * channels, 3 * rows, cols), F32),
            pltpu.VMEM((6 * hid, 256), BF16),
            pltpu.VMEM((wmid.shape[0], 6 * hid, 4 * hid), BF16),
            pltpu.VMEM((3 * channels * rows, (rows + 2) * hid), BF16),
            pltpu.VMEM((18 * hid, cols), BF16),
            pltpu.VMEM((16 * hid, cols), BF16),
            pltpu.VMEM((channels, rows, cols), F32),
            pltpu.SemaphoreType.DMA((2,)),
            pltpu.SemaphoreType.DMA((2,)),
            pltpu.SemaphoreType.DMA((channels,)),
            pltpu.SemaphoreType.DMA((channels,)),
        ],
        compiler_params=pltpu.CompilerParams(
            collective_id=0, has_side_effects=True, vmem_limit_bytes=32 * 2**20
        ),
    )(prev, obs, bounds, factor, time_weight[None], win, wmid, wout)


def solution(mesh):
    placed = (P("tm", None, "strip", None), P(None, "strip", None), P(), P(), P(), P(), P(), P())
    return jax.shard_map(
        functools.partial(on_device, mesh.shape["tm"], mesh.shape["strip"]),
        mesh=mesh,
        in_specs=placed,
        out_specs=P("tm", None, "strip", None),
        check_vma=False,
    )
```

```python
import functools

import jax
import jax.numpy as jnp
from jax import lax
from jax.experimental import pallas as pl
from jax.experimental.pallas import tpu as pltpu
from jax.sharding import PartitionSpec as P

STEPS = 1000
MESH = pl.DeviceIdType.MESH
F32 = jnp.float32
BF16 = jnp.bfloat16


def kernel(
    slices,
    strips,
    *refs,
):
    operands, (out_ref, *local), refs = refs[:8], refs[8:17], refs[17:]
    prev_ref, obs_ref, bounds_ref, factor_ref, time_ref, win_ref, wmid_ref, wout_ref = local
    (
        load_sem,
        own,
        above,
        below,
        field,
        w_first,
        w_mid,
        w_last,
        hidden_a,
        hidden_b,
        arrived,
        halo_send,
        halo_recv,
        relay_send,
        relay_recv,
    ) = refs

    loads = [
        pltpu.make_async_copy(source, place, load_sem.at[k])
        for k, (source, place) in enumerate(zip(operands, local))
    ]
    for load in loads:
        load.start()
    t = lax.axis_index("tm")
    s = lax.axis_index("strip")
    channels, rows, cols = prev_ref.shape[1:]
    hid = time_ref.shape[1]
    middle = wmid_ref.shape[0]
    not_top, not_bottom = s > 0, s < strips - 1
    not_first, not_last = t > 0, t < slices - 1

    barrier = pltpu.get_barrier_semaphore()

    def greet(tt, ss):
        pl.semaphore_signal(barrier, inc=1, device_id=(tt, ss), device_id_type=MESH)

    pl.when(not_top)(lambda: greet(t, s - 1))
    pl.when(not_bottom)(lambda: greet(t, s + 1))
    pl.when(not_first)(lambda: greet(t - 1, s))
    pl.when(not_last)(lambda: greet(t + 1, s))

    loads[0].wait()
    loads[1].wait()
    for c in range(channels):
        field[c, rows : 2 * rows, :] = prev_ref[0, c]
        field[channels + c, rows : 2 * rows, :] = obs_ref[c].astype(F32)
    own[...] = field[:, rows : 2 * rows, :].reshape(2 * channels * rows, cols).astype(BF16)

    greeted = (
        not_top.astype(jnp.int32)
        + not_bottom.astype(jnp.int32)
        + not_first.astype(jnp.int32)
        + not_last.astype(jnp.int32)
    )
    pl.semaphore_wait(barrier, greeted)

    def to_above():
        return pltpu.make_async_remote_copy(
            own, below, halo_send.at[0], halo_recv.at[1], (t, s - 1), MESH
        )

    def to_below():
        return pltpu.make_async_remote_copy(
            own, above, halo_send.at[1], halo_recv.at[0], (t, s + 1), MESH
        )

    pl.when(not_top)(lambda: to_above().start())
    pl.when(not_bottom)(lambda: to_below().start())

    for load in loads[2:]:
        load.wait()
    lane = lax.broadcasted_iota(jnp.int32, (2 * channels, 256), 1)
    chan = lax.broadcasted_iota(jnp.int32, (2 * channels, 256), 0)
    base = jnp.zeros((hid, 256), F32)
    for i in range(3):
        for j in range(3):
            pick = (lane == j * 64 + chan * 8 + i).astype(F32).astype(BF16)
            base = base + lax.dot_general(
                win_ref[i, j], pick, (((0,), (0,)), ((), ())), preferred_element_type=F32
            )
    base = base * 0.5
    for b in range(6):
        turned = pltpu.roll(base, b, 1) if b else base
        w_first[b * hid : (b + 1) * hid, :] = turned.astype(BF16)

    half = jnp.asarray(0.5, BF16)
    none = jnp.zeros((hid, hid), BF16)
    for level in range(middle):
        for j in range(3):
            w = [wmid_ref[level, i, j] * half for i in range(3)]
            at = 2 * j * hid
            w_mid[level, at : at + hid, :] = jnp.concatenate(w + [none], axis=1)
            w_mid[level, at + hid : at + 2 * hid, :] = jnp.concatenate([none] + w, axis=1)

    block = lax.broadcasted_iota(jnp.int32, (rows, 128), 1) // hid
    row_at = lax.broadcasted_iota(jnp.int32, (rows, 128), 0)
    for j in range(3):
        taps = []
        for i in range(3):
            tap = wout_ref[i, j].astype(F32)
            taps.append(jnp.concatenate([tap, tap], axis=1))
        for tile in range((rows + 2) * hid // 128):
            diff = block + 2 * tile - row_at
            parts = []
            for o in range(channels):
                part = jnp.zeros((rows, 128), F32)
                for i in range(3):
                    spread = jnp.broadcast_to(taps[i][o : o + 1], (rows, 128))
                    part = jnp.where(diff == i, spread, part)
                parts.append(part)
            w_last[
                j * channels * rows : (j + 1) * channels * rows, tile * 128 : (tile + 1) * 128
            ] = jnp.concatenate(parts, axis=0).astype(BF16)

    begin = bounds_ref[t].astype(F32)
    finish = bounds_ref[t + 1].astype(F32)
    time_now = begin / STEPS
    time_step = (finish - begin) / STEPS
    eye = lax.broadcasted_iota(jnp.int32, (hid, hid), 0) == lax.broadcasted_iota(
        jnp.int32, (hid, hid), 1
    )
    spread = jnp.broadcast_to(time_ref[...], (hid, hid))
    column = jnp.sum(jnp.where(eye, spread, 0.0), axis=1, keepdims=True)
    bias = (0.5 * time_now) * column

    keep_top = not_top.astype(F32)
    keep_bottom = not_bottom.astype(F32)

    def activated(u, row):
        h = u + u * jnp.tanh(u)
        if row < rows:
            h = h * keep_top
        elif row >= 2 * rows:
            h = h * keep_bottom
        return h.astype(BF16)

    def from_left(v):
        at = lax.broadcasted_iota(jnp.int32, v.shape, 1)
        return jnp.where(at == 0, 0.0, pltpu.roll(v, 1, 1))

    def from_right(v):
        at = lax.broadcasted_iota(jnp.int32, v.shape, 1)
        return jnp.where(at == cols - 1, 0.0, pltpu.roll(v, cols - 1, 1))

    def first_layer(group):
        start = 2 + 6 * group
        window = field[:, start : start + 8, :].reshape(16 * channels, cols)
        stacked = jnp.concatenate(
            [from_left(window).astype(BF16), window.astype(BF16), from_right(window).astype(BF16)],
            axis=0,
        )
        got = jnp.dot(w_first[:, : 3 * 64], stacked, preferred_element_type=F32)
        for b in range(6):
            u = got[b * hid : (b + 1) * hid] + bias
            at = (6 * group + b) * hid
            hidden_a[at : at + hid, :] = activated(u, start + 1 + b)

    first_layer(1)

    @pl.when(not_top)
    def _():
        to_above().wait_send()
        to_below_recv = pltpu.make_async_remote_copy(
            own, above, halo_send.at[1], halo_recv.at[0], (t, s - 1), MESH
        )
        to_below_recv.wait_recv()

    @pl.when(not_bottom)
    def _():
        to_below().wait_send()
        to_above_recv = pltpu.make_async_remote_copy(
            own, below, halo_send.at[0], halo_recv.at[1], (t, s + 1), MESH
        )
        to_above_recv.wait_recv()

    @pl.when(s == 0)
    def _():
        above[...] = jnp.zeros_like(above)

    @pl.when(s == strips - 1)
    def _():
        below[...] = jnp.zeros_like(below)

    field[:, :rows, :] = above[...].astype(F32).reshape(2 * channels, rows, cols)
    field[:, 2 * rows : 3 * rows, :] = below[...].astype(F32).reshape(2 * channels, rows, cols)
    first_layer(0)
    first_layer(2)

    source, target = hidden_a, hidden_b
    for level in range(middle):
        pairs = 8 - level
        for p in range(pairs):
            got = jnp.dot(
                w_mid[level],
                source[p * 2 * hid : p * 2 * hid + 4 * hid, :],
                preferred_element_type=F32,
            )
            u = (
                from_left(got[: 2 * hid])
                + got[2 * hid : 4 * hid]
                + from_right(got[4 * hid :])
            )
            for b in range(2):
                at = (2 * p + b) * hid
                target[at : at + hid, :] = activated(
                    u[b * hid : (b + 1) * hid], 4 + level + 2 * p + b
                )
        source, target = target, source

    count = channels * rows
    got = jnp.dot(w_last[...], source[: (rows + 2) * hid, :], preferred_element_type=F32)
    velocity = from_left(got[:count]) + got[count : 2 * count] + from_right(got[2 * count :])

    def onward(c):
        return pltpu.make_async_remote_copy(
            out_ref.at[0, c], arrived.at[c], relay_send.at[c], relay_recv.at[c], (t + 1, s), MESH
        )

    def backward(c):
        return pltpu.make_async_remote_copy(
            out_ref.at[0, c], arrived.at[c], relay_send.at[c], relay_recv.at[c], (t - 1, s), MESH
        )

    for c in range(channels):
        state = prev_ref[0, c]
        out_ref[0, c] = state + time_step * velocity[c * rows : (c + 1) * rows]

    for c in range(channels):

        @pl.when(not_first)
        def _():
            backward(c).wait_recv()
            out_ref[0, c] = out_ref[0, c] + factor_ref[t, c] * (arrived[c] - prev_ref[0, c])

        pl.when(not_last)(lambda: onward(c).start())

    @pl.when(not_last)
    def _():
        for c in range(channels):
            onward(c).wait_send()


def on_device(slices, strips, *args):
    prev, obs, bounds, factor, time_weight, win, wmid, wout = args
    channels, rows, cols = prev.shape[1:]
    hid = time_weight.shape[0]
    operands = (prev, obs, bounds, factor, time_weight[None])
    operands += (win.transpose(0, 1, 3, 2), wmid, wout)
    local = [
        (pltpu.SMEM if a is bounds or a is factor else pltpu.VMEM)(a.shape, a.dtype)
        for a in operands
    ]
    return pl.pallas_call(
        functools.partial(kernel, slices, strips),
        out_shape=jax.ShapeDtypeStruct(prev.shape, F32),
        in_specs=[pl.BlockSpec(memory_space=pltpu.HBM)] * len(operands),
        out_specs=pl.BlockSpec(memory_space=pltpu.VMEM),
        scratch_shapes=[
            *local,
            pltpu.SemaphoreType.DMA((len(operands),)),
            pltpu.VMEM((2 * channels * rows, cols), BF16),
            pltpu.VMEM((2 * channels * rows, cols), BF16),
            pltpu.VMEM((2 * channels * rows, cols), BF16),
            pltpu.VMEM((2 * channels, 3 * rows, cols), F32),
            pltpu.VMEM((6 * hid, 256), BF16),
            pltpu.VMEM((wmid.shape[0], 6 * hid, 4 * hid), BF16),
            pltpu.VMEM((3 * channels * rows, (rows + 2) * hid), BF16),
            pltpu.VMEM((18 * hid, cols), BF16),
            pltpu.VMEM((16 * hid, cols), BF16),
            pltpu.VMEM((channels, rows, cols), F32),
            pltpu.SemaphoreType.DMA((2,)),
            pltpu.SemaphoreType.DMA((2,)),
            pltpu.SemaphoreType.DMA((channels,)),
            pltpu.SemaphoreType.DMA((channels,)),
        ],
        compiler_params=pltpu.CompilerParams(
            collective_id=0, has_side_effects=True, vmem_limit_bytes=60 * 2**20
        ),
    )(*operands)


def solution(mesh):
    placed = (P("tm", None, "strip", None), P(None, "strip", None), P(), P(), P(), P(), P(), P())
    return jax.shard_map(
        functools.partial(on_device, mesh.shape["tm"], mesh.shape["strip"]),
        mesh=mesh,
        in_specs=placed,
        out_specs=P("tm", None, "strip", None),
        check_vma=False,
    )
```

```python
import functools

import jax
import jax.numpy as jnp
from jax import lax
from jax.experimental import pallas as pl
from jax.experimental.pallas import tpu as pltpu
from jax.sharding import PartitionSpec as P

STEPS = 1000
MESH = pl.DeviceIdType.MESH
F32 = jnp.float32
BF16 = jnp.bfloat16


def kernel(
    slices,
    strips,
    *refs,
):
    operands, (out_ref, *local), refs = refs[:8], refs[8:17], refs[17:]
    prev_ref, obs_ref, bounds_ref, factor_ref, time_ref, win_ref, wmid_ref, wout_ref = local
    (
        load_sem,
        own,
        above,
        below,
        field,
        w_first,
        w_mid,
        w_last,
        hidden_a,
        hidden_b,
        speed,
        states,
        speeds,
        halo_send,
        halo_recv,
        state_send,
        state_recv,
        speed_send,
        speed_recv,
    ) = refs

    loads = [
        pltpu.make_async_copy(source, place, load_sem.at[k])
        for k, (source, place) in enumerate(zip(operands, local))
    ]
    for load in loads:
        load.start()
    t = lax.axis_index("tm")
    s = lax.axis_index("strip")
    channels, rows, cols = prev_ref.shape[1:]
    hid = time_ref.shape[1]
    middle = wmid_ref.shape[0]
    not_top, not_bottom = s > 0, s < strips - 1

    barrier = pltpu.get_barrier_semaphore()

    def greet(tt, ss):
        pl.semaphore_signal(barrier, inc=1, device_id=(tt, ss), device_id_type=MESH)

    pl.when(not_top)(lambda: greet(t, s - 1))
    pl.when(not_bottom)(lambda: greet(t, s + 1))
    for k in range(1, slices):
        greet(lax.rem(t + k, slices), s)

    loads[0].wait()
    loads[1].wait()
    for c in range(channels):
        field[c, rows : 2 * rows, :] = prev_ref[0, c]
        field[channels + c, rows : 2 * rows, :] = obs_ref[c].astype(F32)
    own[...] = field[:, rows : 2 * rows, :].reshape(2 * channels * rows, cols).astype(BF16)

    greeted = (
        not_top.astype(jnp.int32) + not_bottom.astype(jnp.int32) + (slices - 1)
    )
    pl.semaphore_wait(barrier, greeted)

    def to_above():
        return pltpu.make_async_remote_copy(
            own, below, halo_send.at[0], halo_recv.at[1], (t, s - 1), MESH
        )

    def to_below():
        return pltpu.make_async_remote_copy(
            own, above, halo_send.at[1], halo_recv.at[0], (t, s + 1), MESH
        )

    pl.when(not_top)(lambda: to_above().start())
    pl.when(not_bottom)(lambda: to_below().start())

    def state_copy(k, to):
        return pltpu.make_async_remote_copy(
            prev_ref, states.at[k - 1], state_send.at[k - 1], state_recv.at[k - 1], (to, s), MESH
        )

    def speed_copy(k, to):
        return pltpu.make_async_remote_copy(
            speed, speeds.at[k - 1], speed_send.at[k - 1], speed_recv.at[k - 1], (to, s), MESH
        )

    for k in reversed(range(1, slices)):
        pl.when(t + k < slices)(lambda: state_copy(k, t + k).start())

    for load in loads[2:]:
        load.wait()
    lane = lax.broadcasted_iota(jnp.int32, (2 * channels, 256), 1)
    chan = lax.broadcasted_iota(jnp.int32, (2 * channels, 256), 0)
    base = jnp.zeros((hid, 256), F32)
    for i in range(3):
        for j in range(3):
            pick = (lane == j * 64 + chan * 8 + i).astype(F32).astype(BF16)
            base = base + lax.dot_general(
                win_ref[i, j], pick, (((0,), (0,)), ((), ())), preferred_element_type=F32
            )
    base = base * 0.5
    for b in range(6):
        turned = pltpu.roll(base, b, 1) if b else base
        w_first[b * hid : (b + 1) * hid, :] = turned.astype(BF16)

    half = jnp.asarray(0.5, BF16)
    none = jnp.zeros((hid, hid), BF16)
    for level in range(middle):
        for j in range(3):
            w = [wmid_ref[level, i, j] * half for i in range(3)]
            at = 2 * j * hid
            w_mid[level, at : at + hid, :] = jnp.concatenate(w + [none], axis=1)
            w_mid[level, at + hid : at + 2 * hid, :] = jnp.concatenate([none] + w, axis=1)

    block = lax.broadcasted_iota(jnp.int32, (rows, 128), 1) // hid
    row_at = lax.broadcasted_iota(jnp.int32, (rows, 128), 0)
    for j in range(3):
        taps = []
        for i in range(3):
            tap = wout_ref[i, j].astype(F32)
            taps.append(jnp.concatenate([tap, tap], axis=1))
        for tile in range((rows + 2) * hid // 128):
            diff = block + 2 * tile - row_at
            parts = []
            for o in range(channels):
                part = jnp.zeros((rows, 128), F32)
                for i in range(3):
                    spread = jnp.broadcast_to(taps[i][o : o + 1], (rows, 128))
                    part = jnp.where(diff == i, spread, part)
                parts.append(part)
            w_last[
                j * channels * rows : (j + 1) * channels * rows, tile * 128 : (tile + 1) * 128
            ] = jnp.concatenate(parts, axis=0).astype(BF16)

    begin = bounds_ref[t].astype(F32)
    finish = bounds_ref[t + 1].astype(F32)
    time_now = begin / STEPS
    time_step = (finish - begin) / STEPS
    eye = lax.broadcasted_iota(jnp.int32, (hid, hid), 0) == lax.broadcasted_iota(
        jnp.int32, (hid, hid), 1
    )
    spread = jnp.broadcast_to(time_ref[...], (hid, hid))
    column = jnp.sum(jnp.where(eye, spread, 0.0), axis=1, keepdims=True)
    bias = (0.5 * time_now) * column

    keep_top = not_top.astype(F32)
    keep_bottom = not_bottom.astype(F32)

    def activated(u, row):
        h = u + u * jnp.tanh(u)
        if row < rows:
            h = h * keep_top
        elif row >= 2 * rows:
            h = h * keep_bottom
        return h.astype(BF16)

    def from_left(v):
        at = lax.broadcasted_iota(jnp.int32, v.shape, 1)
        return jnp.where(at == 0, 0.0, pltpu.roll(v, 1, 1))

    def from_right(v):
        at = lax.broadcasted_iota(jnp.int32, v.shape, 1)
        return jnp.where(at == cols - 1, 0.0, pltpu.roll(v, cols - 1, 1))

    def first_layer(group):
        start = 2 + 6 * group
        window = field[:, start : start + 8, :].reshape(16 * channels, cols)
        stacked = jnp.concatenate(
            [from_left(window).astype(BF16), window.astype(BF16), from_right(window).astype(BF16)],
            axis=0,
        )
        got = jnp.dot(w_first[:, : 3 * 64], stacked, preferred_element_type=F32)
        for b in range(6):
            u = got[b * hid : (b + 1) * hid] + bias
            at = (6 * group + b) * hid
            hidden_a[at : at + hid, :] = activated(u, start + 1 + b)

    first_layer(1)

    @pl.when(not_top)
    def _():
        to_above().wait_send()
        to_below_recv = pltpu.make_async_remote_copy(
            own, above, halo_send.at[1], halo_recv.at[0], (t, s - 1), MESH
        )
        to_below_recv.wait_recv()

    @pl.when(not_bottom)
    def _():
        to_below().wait_send()
        to_above_recv = pltpu.make_async_remote_copy(
            own, below, halo_send.at[0], halo_recv.at[1], (t, s + 1), MESH
        )
        to_above_recv.wait_recv()

    @pl.when(s == 0)
    def _():
        above[...] = jnp.zeros_like(above)

    @pl.when(s == strips - 1)
    def _():
        below[...] = jnp.zeros_like(below)

    field[:, :rows, :] = above[...].astype(F32).reshape(2 * channels, rows, cols)
    field[:, 2 * rows : 3 * rows, :] = below[...].astype(F32).reshape(2 * channels, rows, cols)
    first_layer(0)
    first_layer(2)

    source, target = hidden_a, hidden_b
    for level in range(middle):
        pairs = 8 - level
        for p in range(pairs):
            got = jnp.dot(
                w_mid[level],
                source[p * 2 * hid : p * 2 * hid + 4 * hid, :],
                preferred_element_type=F32,
            )
            u = (
                from_left(got[: 2 * hid])
                + got[2 * hid : 4 * hid]
                + from_right(got[4 * hid :])
            )
            for b in range(2):
                at = (2 * p + b) * hid
                target[at : at + hid, :] = activated(
                    u[b * hid : (b + 1) * hid], 4 + level + 2 * p + b
                )
        source, target = target, source

    count = channels * rows
    got = jnp.dot(w_last[...], source[: (rows + 2) * hid, :], preferred_element_type=F32)
    velocity = from_left(got[:count]) + got[count : 2 * count] + from_right(got[2 * count :])

    speed[...] = velocity.astype(BF16)
    for k in reversed(range(1, slices)):
        pl.when(t + k < slices)(lambda: speed_copy(k, t + k).start())

    keep = (t > 0).astype(F32)
    for c in range(channels):
        moved = time_step * velocity[c * rows : (c + 1) * rows]
        out_ref[0, c] = (1.0 - keep * factor_ref[t, c]) * prev_ref[0, c] + moved

    def decay(k, c):
        product = factor_ref[t, c]
        for back in range(1, k):
            product = product * factor_ref[jnp.maximum(t - back, 0), c]
        return product

    for k in range(1, slices):

        @pl.when(t >= k)
        def _():
            state_copy(k, t - k).wait_recv()
            keep = (t > k).astype(F32)
            for c in range(channels):
                scale = decay(k, c) * (1.0 - keep * factor_ref[jnp.maximum(t - k, 0), c])
                out_ref[0, c] = out_ref[0, c] + scale * states[k - 1, 0, c]

    for k in range(1, slices):

        @pl.when(t >= k)
        def _():
            origin = jnp.maximum(t - k, 0)
            step = (bounds_ref[origin + 1] - bounds_ref[origin]).astype(F32) / STEPS
            speed_copy(k, t - k).wait_recv()
            taken = speeds[k - 1].astype(F32)
            for c in range(channels):
                part = taken[c * rows : (c + 1) * rows]
                out_ref[0, c] = out_ref[0, c] + (decay(k, c) * step) * part

    for k in range(1, slices):

        @pl.when(t + k < slices)
        def _():
            state_copy(k, t + k).wait_send()
            speed_copy(k, t + k).wait_send()


def on_device(slices, strips, *args):
    prev, obs, bounds, factor, time_weight, win, wmid, wout = args
    channels, rows, cols = prev.shape[1:]
    hid = time_weight.shape[0]
    operands = (prev, obs, bounds, factor, time_weight[None])
    operands += (win.transpose(0, 1, 3, 2), wmid, wout)
    local = [
        (pltpu.SMEM if a is bounds or a is factor else pltpu.VMEM)(a.shape, a.dtype)
        for a in operands
    ]
    return pl.pallas_call(
        functools.partial(kernel, slices, strips),
        out_shape=jax.ShapeDtypeStruct(prev.shape, F32),
        in_specs=[pl.BlockSpec(memory_space=pltpu.HBM)] * len(operands),
        out_specs=pl.BlockSpec(memory_space=pltpu.VMEM),
        scratch_shapes=[
            *local,
            pltpu.SemaphoreType.DMA((len(operands),)),
            pltpu.VMEM((2 * channels * rows, cols), BF16),
            pltpu.VMEM((2 * channels * rows, cols), BF16),
            pltpu.VMEM((2 * channels * rows, cols), BF16),
            pltpu.VMEM((2 * channels, 3 * rows, cols), F32),
            pltpu.VMEM((6 * hid, 256), BF16),
            pltpu.VMEM((wmid.shape[0], 6 * hid, 4 * hid), BF16),
            pltpu.VMEM((3 * channels * rows, (rows + 2) * hid), BF16),
            pltpu.VMEM((18 * hid, cols), BF16),
            pltpu.VMEM((16 * hid, cols), BF16),
            pltpu.VMEM((channels * rows, cols), BF16),
            pltpu.VMEM((slices - 1, *prev.shape), F32),
            pltpu.VMEM((slices - 1, channels * rows, cols), BF16),
            pltpu.SemaphoreType.DMA((2,)),
            pltpu.SemaphoreType.DMA((2,)),
            pltpu.SemaphoreType.DMA((slices - 1,)),
            pltpu.SemaphoreType.DMA((slices - 1,)),
            pltpu.SemaphoreType.DMA((slices - 1,)),
            pltpu.SemaphoreType.DMA((slices - 1,)),
        ],
        compiler_params=pltpu.CompilerParams(
            collective_id=0, has_side_effects=True, vmem_limit_bytes=60 * 2**20
        ),
    )(*operands)


def solution(mesh):
    placed = (P("tm", None, "strip", None), P(None, "strip", None), P(), P(), P(), P(), P(), P())
    return jax.shard_map(
        functools.partial(on_device, mesh.shape["tm"], mesh.shape["strip"]),
        mesh=mesh,
        in_specs=placed,
        out_specs=P("tm", None, "strip", None),
        check_vma=False,
    )
```

```python
import functools

import jax
import jax.numpy as jnp
from jax import lax
from jax.experimental import pallas as pl
from jax.experimental.pallas import tpu as pltpu
from jax.sharding import PartitionSpec as P

STEPS = 1000
MESH = pl.DeviceIdType.MESH
F32 = jnp.float32
BF16 = jnp.bfloat16


def kernel(
    slices,
    strips,
    *refs,
):
    operands, (out_ref, *local), refs = refs[:8], refs[8:17], refs[17:]
    prev_ref, obs_ref, bounds_ref, factor_ref, time_ref, win_ref, wmid_ref, wout_ref = local
    (
        load_sem,
        own,
        above,
        below,
        field,
        w_first,
        w_mid,
        w_last,
        hidden_a,
        hidden_b,
        speed,
        states,
        speeds,
        halo_send,
        halo_recv,
        state_send,
        state_recv,
        speed_send,
        speed_recv,
    ) = refs

    loads = [
        pltpu.make_async_copy(source, place, load_sem.at[k])
        for k, (source, place) in enumerate(zip(operands, local))
    ]
    for load in loads:
        load.start()
    t = lax.axis_index("tm")
    s = lax.axis_index("strip")
    channels, rows, cols = prev_ref.shape[1:]
    hid = time_ref.shape[1]
    middle = wmid_ref.shape[0]
    not_top, not_bottom = s > 0, s < strips - 1

    barrier = pltpu.get_barrier_semaphore()

    def greet(tt, ss):
        pl.semaphore_signal(barrier, inc=1, device_id=(tt, ss), device_id_type=MESH)

    pl.when(not_top)(lambda: greet(t, s - 1))
    pl.when(not_bottom)(lambda: greet(t, s + 1))
    for k in range(1, slices):
        greet(lax.rem(t + k, slices), s)

    loads[0].wait()
    loads[1].wait()
    for c in range(channels):
        field[c, rows : 2 * rows, :] = prev_ref[0, c]
        field[channels + c, rows : 2 * rows, :] = obs_ref[c].astype(F32)
    own[...] = field[:, rows : 2 * rows, :].reshape(2 * channels * rows, cols).astype(BF16)

    greeted = (
        not_top.astype(jnp.int32) + not_bottom.astype(jnp.int32) + (slices - 1)
    )
    pl.semaphore_wait(barrier, greeted)

    def to_above():
        return pltpu.make_async_remote_copy(
            own, below, halo_send.at[0], halo_recv.at[1], (t, s - 1), MESH
        )

    def to_below():
        return pltpu.make_async_remote_copy(
            own, above, halo_send.at[1], halo_recv.at[0], (t, s + 1), MESH
        )

    pl.when(not_top)(lambda: to_above().start())
    pl.when(not_bottom)(lambda: to_below().start())

    def state_copy(k, to):
        return pltpu.make_async_remote_copy(
            prev_ref, states.at[k - 1], state_send.at[k - 1], state_recv.at[k - 1], (to, s), MESH
        )

    def speed_copy(k, to):
        return pltpu.make_async_remote_copy(
            speed, speeds.at[k - 1], speed_send.at[k - 1], speed_recv.at[k - 1], (to, s), MESH
        )

    for k in reversed(range(1, slices)):
        pl.when(t + k < slices)(lambda: state_copy(k, t + k).start())

    for load in loads[2:]:
        load.wait()
    lane = lax.broadcasted_iota(jnp.int32, (2 * channels, 256), 1)
    chan = lax.broadcasted_iota(jnp.int32, (2 * channels, 256), 0)
    base = jnp.zeros((hid, 256), F32)
    for i in range(3):
        for j in range(3):
            pick = (lane == j * 64 + chan * 8 + i).astype(F32).astype(BF16)
            base = base + lax.dot_general(
                win_ref[i, j], pick, (((0,), (0,)), ((), ())), preferred_element_type=F32
            )
    base = base * 0.5
    for b in range(6):
        turned = pltpu.roll(base, b, 1) if b else base
        w_first[b * hid : (b + 1) * hid, :] = turned.astype(BF16)

    half = jnp.asarray(0.5, BF16)
    none = jnp.zeros((hid, hid), BF16)
    for level in range(middle):
        for j in range(3):
            w = [wmid_ref[level, i, j] * half for i in range(3)]
            at = 2 * j * hid
            w_mid[level, at : at + hid, :] = jnp.concatenate(w + [none], axis=1)
            w_mid[level, at + hid : at + 2 * hid, :] = jnp.concatenate([none] + w, axis=1)

    block = lax.broadcasted_iota(jnp.int32, (rows, 128), 1) // hid
    row_at = lax.broadcasted_iota(jnp.int32, (rows, 128), 0)
    for j in range(3):
        taps = []
        for i in range(3):
            tap = wout_ref[i, j].astype(F32)
            taps.append(jnp.concatenate([tap, tap], axis=1))
        for tile in range((rows + 2) * hid // 128):
            diff = block + 2 * tile - row_at
            parts = []
            for o in range(channels):
                part = jnp.zeros((rows, 128), F32)
                for i in range(3):
                    spread = jnp.broadcast_to(taps[i][o : o + 1], (rows, 128))
                    part = jnp.where(diff == i, spread, part)
                parts.append(part)
            w_last[
                j * channels * rows : (j + 1) * channels * rows, tile * 128 : (tile + 1) * 128
            ] = jnp.concatenate(parts, axis=0).astype(BF16)

    begin = bounds_ref[t].astype(F32)
    finish = bounds_ref[t + 1].astype(F32)
    time_now = begin / STEPS
    time_step = (finish - begin) / STEPS
    eye = lax.broadcasted_iota(jnp.int32, (hid, hid), 0) == lax.broadcasted_iota(
        jnp.int32, (hid, hid), 1
    )
    spread = jnp.broadcast_to(time_ref[...], (hid, hid))
    column = jnp.sum(jnp.where(eye, spread, 0.0), axis=1, keepdims=True)
    bias = (0.5 * time_now) * column

    keep_top = not_top.astype(F32)
    keep_bottom = not_bottom.astype(F32)

    def activated(u, row):
        h = u + u * jnp.tanh(u)
        if row < rows:
            h = h * keep_top
        elif row >= 2 * rows:
            h = h * keep_bottom
        return h.astype(BF16)

    def from_left(v):
        at = lax.broadcasted_iota(jnp.int32, v.shape, 1)
        return jnp.where(at == 0, 0.0, pltpu.roll(v, 1, 1))

    def from_right(v):
        at = lax.broadcasted_iota(jnp.int32, v.shape, 1)
        return jnp.where(at == cols - 1, 0.0, pltpu.roll(v, cols - 1, 1))

    def first_layer(group):
        start = 2 + 6 * group
        window = field[:, start : start + 8, :].reshape(16 * channels, cols)
        stacked = jnp.concatenate(
            [from_left(window).astype(BF16), window.astype(BF16), from_right(window).astype(BF16)],
            axis=0,
        )
        got = jnp.dot(w_first[:, : 3 * 64], stacked, preferred_element_type=F32)
        for b in range(6):
            u = got[b * hid : (b + 1) * hid] + bias
            at = (6 * group + b) * hid
            hidden_a[at : at + hid, :] = activated(u, start + 1 + b)

    def middle_pair(level, p, source, target):
        got = jnp.dot(
            w_mid[level],
            source[p * 2 * hid : p * 2 * hid + 4 * hid, :],
            preferred_element_type=F32,
        )
        u = from_left(got[: 2 * hid]) + got[2 * hid : 4 * hid] + from_right(got[4 * hid :])
        for b in range(2):
            at = (2 * p + b) * hid
            target[at : at + hid, :] = activated(u[b * hid : (b + 1) * hid], 4 + level + 2 * p + b)

    first_layer(1)
    inner = (3, 4)
    for p in inner:
        middle_pair(0, p, hidden_a, hidden_b)

    @pl.when(not_top)
    def _():
        to_above().wait_send()
        to_below_recv = pltpu.make_async_remote_copy(
            own, above, halo_send.at[1], halo_recv.at[0], (t, s - 1), MESH
        )
        to_below_recv.wait_recv()

    @pl.when(not_bottom)
    def _():
        to_below().wait_send()
        to_above_recv = pltpu.make_async_remote_copy(
            own, below, halo_send.at[0], halo_recv.at[1], (t, s + 1), MESH
        )
        to_above_recv.wait_recv()

    @pl.when(s == 0)
    def _():
        above[...] = jnp.zeros_like(above)

    @pl.when(s == strips - 1)
    def _():
        below[...] = jnp.zeros_like(below)

    field[:, :rows, :] = above[...].astype(F32).reshape(2 * channels, rows, cols)
    field[:, 2 * rows : 3 * rows, :] = below[...].astype(F32).reshape(2 * channels, rows, cols)
    first_layer(0)
    first_layer(2)

    source, target = hidden_a, hidden_b
    for level in range(middle):
        for p in range(8 - level):
            if level or p not in inner:
                middle_pair(level, p, source, target)
        source, target = target, source

    count = channels * rows
    got = jnp.dot(w_last[...], source[: (rows + 2) * hid, :], preferred_element_type=F32)
    velocity = from_left(got[:count]) + got[count : 2 * count] + from_right(got[2 * count :])

    speed[...] = velocity.astype(BF16)
    for k in reversed(range(1, slices)):
        pl.when(t + k < slices)(lambda: speed_copy(k, t + k).start())

    keep = (t > 0).astype(F32)
    for c in range(channels):
        moved = time_step * velocity[c * rows : (c + 1) * rows]
        out_ref[0, c] = (1.0 - keep * factor_ref[t, c]) * prev_ref[0, c] + moved

    def decay(k, c):
        product = factor_ref[t, c]
        for back in range(1, k):
            product = product * factor_ref[jnp.maximum(t - back, 0), c]
        return product

    for k in range(1, slices):

        @pl.when(t >= k)
        def _():
            state_copy(k, t - k).wait_recv()
            keep = (t > k).astype(F32)
            for c in range(channels):
                scale = decay(k, c) * (1.0 - keep * factor_ref[jnp.maximum(t - k, 0), c])
                out_ref[0, c] = out_ref[0, c] + scale * states[k - 1, 0, c]

    for k in range(1, slices):

        @pl.when(t >= k)
        def _():
            origin = jnp.maximum(t - k, 0)
            step = (bounds_ref[origin + 1] - bounds_ref[origin]).astype(F32) / STEPS
            speed_copy(k, t - k).wait_recv()
            taken = speeds[k - 1].astype(F32)
            for c in range(channels):
                part = taken[c * rows : (c + 1) * rows]
                out_ref[0, c] = out_ref[0, c] + (decay(k, c) * step) * part

    for k in range(1, slices):

        @pl.when(t + k < slices)
        def _():
            state_copy(k, t + k).wait_send()
            speed_copy(k, t + k).wait_send()


def on_device(slices, strips, *args):
    prev, obs, bounds, factor, time_weight, win, wmid, wout = args
    channels, rows, cols = prev.shape[1:]
    hid = time_weight.shape[0]
    operands = (prev, obs, bounds, factor, time_weight[None])
    operands += (win.transpose(0, 1, 3, 2), wmid, wout)
    local = [
        (pltpu.SMEM if a is bounds or a is factor else pltpu.VMEM)(a.shape, a.dtype)
        for a in operands
    ]
    return pl.pallas_call(
        functools.partial(kernel, slices, strips),
        out_shape=jax.ShapeDtypeStruct(prev.shape, F32),
        in_specs=[pl.BlockSpec(memory_space=pltpu.HBM)] * len(operands),
        out_specs=pl.BlockSpec(memory_space=pltpu.VMEM),
        scratch_shapes=[
            *local,
            pltpu.SemaphoreType.DMA((len(operands),)),
            pltpu.VMEM((2 * channels * rows, cols), BF16),
            pltpu.VMEM((2 * channels * rows, cols), BF16),
            pltpu.VMEM((2 * channels * rows, cols), BF16),
            pltpu.VMEM((2 * channels, 3 * rows, cols), F32),
            pltpu.VMEM((6 * hid, 256), BF16),
            pltpu.VMEM((wmid.shape[0], 6 * hid, 4 * hid), BF16),
            pltpu.VMEM((3 * channels * rows, (rows + 2) * hid), BF16),
            pltpu.VMEM((18 * hid, cols), BF16),
            pltpu.VMEM((16 * hid, cols), BF16),
            pltpu.VMEM((channels * rows, cols), BF16),
            pltpu.VMEM((slices - 1, *prev.shape), F32),
            pltpu.VMEM((slices - 1, channels * rows, cols), BF16),
            pltpu.SemaphoreType.DMA((2,)),
            pltpu.SemaphoreType.DMA((2,)),
            pltpu.SemaphoreType.DMA((slices - 1,)),
            pltpu.SemaphoreType.DMA((slices - 1,)),
            pltpu.SemaphoreType.DMA((slices - 1,)),
            pltpu.SemaphoreType.DMA((slices - 1,)),
        ],
        compiler_params=pltpu.CompilerParams(
            collective_id=0, has_side_effects=True, vmem_limit_bytes=60 * 2**20
        ),
    )(*operands)


def solution(mesh):
    placed = (P("tm", None, "strip", None), P(None, "strip", None), P(), P(), P(), P(), P(), P())
    return jax.shard_map(
        functools.partial(on_device, mesh.shape["tm"], mesh.shape["strip"]),
        mesh=mesh,
        in_specs=placed,
        out_specs=P("tm", None, "strip", None),
        check_vma=False,
    )
```
